32 devices in a mesh: trial: 4 (over y, x), dp: 8 (over z, core).
Axes of the slice: x: 2, y: 2, z: 4, core: 2. Of those that a mesh axis runs over, the one named last changes fastest.
Arguments:
- grads: bfloat16 [32, 4, 512, 512], P(('trial', 'dp')), may hold values from -75 to 75
- exponents: int32 [8], replicated, may hold values from 2 to 4
- dampings: float32 [8], replicated, may hold values from 0.05 to 0.5
Outputs:
- updates: bfloat16 [8, 4, 512, 512], P(None, None, 'dp', 'trial')
The draws below stay inside these ranges and needn't reach their ends.
All inputs are finite; a program needn't handle non-finite values.
Results may differ from the reference program's by a relative error of at most 0.0004.
Values may be sent and summed in bfloat16 or wider, within the bound.
A program may use at most 128 MiB of HBM per device.

```python
import math
import jax
import jax.numpy as jnp
from jax import lax

B = 512
TRIALS = 8
ITERS = 2
NT = 4
MICRO = 32
TASKS = 32


def draw_grads(key, part):
    key = jax.random.fold_in(key, 7)
    subkeys = jax.random.split(key, 4)
    low_end = 0.3
    high_end = 3.0
    common = jax.random.truncated_normal(subkeys[0], -4.0, 4.0, (1, NT, B, B), jnp.float32)
    noise = 0.5 * jax.random.truncated_normal(subkeys[1], -4.0, 4.0, (MICRO, NT, B, B), jnp.float32)
    row_scale = jnp.exp(jax.random.uniform(subkeys[2], (1, NT, B, 1), jnp.float32, math.log(low_end), math.log(high_end)))
    col_scale = jnp.exp(jax.random.uniform(subkeys[3], (1, NT, 1, B), jnp.float32, math.log(low_end), math.log(high_end)))
    return (row_scale * col_scale * (common + noise)).astype(jnp.bfloat16)


def with_ends(result, rng, low, top_value):
    extent = result.shape
    index_at = [jax.random.randint(jax.random.fold_in(rng, axis), (), 0, extent[axis]) for axis in range(len(extent))]
    result = result.at[tuple(index_at)].set(low)
    longest = extent.index(max(extent))
    index_at[longest] = (index_at[longest] + 1) % extent[longest]
    return result.at[tuple(index_at)].set(top_value)


def setup_inputs(seed: int = 0) -> dict:
    keys = jax.random.split(jax.random.key(seed), 4)
    return {
        "grads": draw_grads(jax.random.fold_in(keys[3], 71), 0),
        "exponents": with_ends(jax.random.randint(keys[1], (TRIALS,), 2, 5), jax.random.fold_in(keys[1], 1), 2, 4).astype(jnp.int32),
        "dampings": jnp.clip(jnp.exp(jax.random.uniform(keys[2], (TRIALS,), jnp.float32, math.log(0.05), math.log(0.5))), 0.05, 0.5),
    }


def matmul_full(first_mat, second_mat):
    return jnp.matmul(first_mat, second_mat, precision=lax.Precision.HIGHEST)

def inverse_root(statistic, exponent, damping):
    identity = jnp.eye(statistic.shape[-1], dtype=jnp.float32)
    shifted = statistic + damping * identity
    order_f = exponent.astype(jnp.float32)
    scaling = (1.0 + order_f) / (2.0 * jnp.sqrt(jnp.sum(shifted * shifted) + 1e-06))
    moment = scaling * shifted
    root_now = jnp.exp(jnp.log(scaling) / order_f) * identity
    for iteration in range(ITERS):
        factor = ((order_f + 1.0) * identity - moment) / order_f
        root_now = matmul_full(root_now, factor)
        if iteration + 1 < ITERS:
            raised = lax.fori_loop(1, exponent, lambda turn, product: matmul_full(product, factor), factor)
            moment = matmul_full(raised, moment)
    return root_now

def graft(raw_update, average):
    target = jnp.sqrt(jnp.mean(average * average))
    return raw_update * target / jnp.sqrt(jnp.mean(raw_update * raw_update) + 1e-06)

def reference(grads, exponents, dampings):

    def per_tile(tile_index):
        blocks = lax.dynamic_index_in_dim(grads, tile_index, 1, keepdims=False)
        wide_rows = blocks.transpose(1, 0, 2).reshape(B, MICRO * B)
        tall_rows = blocks.reshape(MICRO * B, B)
        left_stat = jnp.dot(wide_rows, wide_rows.T, preferred_element_type=jnp.float32) / (MICRO * B)
        right_stat = jnp.dot(tall_rows.T, tall_rows, preferred_element_type=jnp.float32) / (MICRO * B)
        average = lax.optimization_barrier(jnp.sum(blocks.astype(jnp.float32), axis=0)) / MICRO
        return (left_stat, right_stat, average)
    lefts, rights, averages = lax.map(per_tile, jnp.arange(NT, dtype=jnp.int32))

    def per_task(task_index):
        trial_index = task_index // NT
        tile_index = task_index % NT
        exponent = exponents[trial_index]
        damping = dampings[trial_index]
        left_root = inverse_root(lefts[tile_index], exponent, damping)
        right_root = inverse_root(rights[tile_index], exponent, damping)
        average = averages[tile_index]
        raw_update = matmul_full(matmul_full(left_root, average), right_root)
        return graft(raw_update, average).astype(jnp.bfloat16)
    updates = lax.map(per_task, jnp.arange(TASKS, dtype=jnp.int32))
    return updates.reshape(TRIALS, NT, B, B)
```

```python
import jax
import jax.numpy as jnp
from jax import lax
from jax.sharding import PartitionSpec as P


def matmul_full(first_mat, second_mat):
    return jnp.matmul(first_mat, second_mat, precision=lax.Precision.HIGHEST)


def inverse_root(statistic, exponent, damping):
    identity = jnp.eye(statistic.shape[-1], dtype=jnp.float32)
    shifted = statistic + damping * identity
    order_f = exponent.astype(jnp.float32)
    scaling = (1.0 + order_f) / (2.0 * jnp.sqrt(jnp.sum(shifted * shifted) + 1e-06))
    factor = ((order_f + 1.0) * identity - scaling * shifted) / order_f
    square = matmul_full(factor, factor)
    cube = matmul_full(square, factor)
    low = jnp.where(exponent == 2, factor, square)
    high = jnp.where(exponent == 2, square, cube)
    outer = jnp.where(exponent == 4, cube, square)
    tail = matmul_full(outer, order_f * high - (order_f + 1.0) * low)
    return jnp.exp(jnp.log(scaling) / order_f) / order_f * ((order_f + 1.0) * factor + tail)


def graft(raw_update, average):
    target = jnp.sqrt(jnp.mean(average * average))
    spread = jnp.sqrt(jnp.mean(raw_update * raw_update) + 1e-06)
    return raw_update * target / spread


def per_device(grads, exponents, dampings):
    trials_n = lax.axis_size("trial")
    data_n = lax.axis_size("dp")
    devices = trials_n * data_n
    settings = exponents.shape[0]
    block_order = grads.shape[-1]
    row_share = block_order // data_n
    col_share = block_order // trials_n
    here_data = lax.axis_index("dp")

    mine = lax.all_to_all(grads[0], "trial", split_axis=0, concat_axis=0, tiled=True)
    weight = 1.0 / (devices * block_order)
    left = jnp.einsum("irk,ick->rc", mine, mine, preferred_element_type=jnp.float32) * weight
    right = jnp.einsum("ikr,ikc->rc", mine, mine, preferred_element_type=jnp.float32) * weight
    average = jnp.sum(mine.astype(jnp.float32), axis=0) * (1.0 / devices)
    statistics, average = lax.psum((jnp.stack([left, right]), average), "dp")

    setting = here_data % settings
    roots = jax.vmap(inverse_root, in_axes=(0, None, None))(
        statistics, exponents[setting], dampings[setting]
    )
    raw_update = matmul_full(matmul_full(roots[0], average), roots[1])
    finished = graft(raw_update, average).astype(jnp.bfloat16)

    blocks = finished.reshape(data_n, row_share, trials_n, col_share).transpose(2, 0, 1, 3)
    returned = lax.all_to_all(
        blocks.reshape(devices, row_share, col_share),
        ("trial", "dp"),
        split_axis=0,
        concat_axis=0,
        tiled=True,
    )
    by_source = returned.reshape(trials_n, data_n, row_share, col_share)
    return by_source[:, :settings].transpose(1, 0, 2, 3)


def solution(mesh):
    placed = (P(("trial", "dp"), None, None, None), P(), P())
    return jax.shard_map(
        per_device,
        mesh=mesh,
        in_specs=placed,
        out_specs=P(None, None, "dp", "trial"),
        check_vma=False,
    )
```

```python
import functools

import jax
import jax.numpy as jnp
from jax import lax
from jax.experimental import pallas as pl
from jax.experimental.pallas import tpu as pltpu
from jax.sharding import PartitionSpec as P

MESH = pl.DeviceIdType.MESH
BANDS = 4
CHUNKS = 6
F32 = jnp.float32
BF16 = jnp.bfloat16


def stat_pieces(order):
    band = order // BANDS
    pieces = []
    for kind in range(2):
        base = kind * 2 * band
        pieces.append((kind, 3, base, 0))
        pieces.append((kind, 2, base + band, 0))
        pieces.append((kind, 0, base + band, 3 * band))
        pieces.append((kind, 1, 4 * band, kind * 2 * band))
    return band, pieces


def packed_rows(order):
    return 5 * (order // BANDS) + order


def add_tile(part, tile, first):
    order = part.shape[1]
    band, pieces = stat_pieces(order)
    for kind, index, row, col in pieces:
        width = (index + 1) * band
        if kind == 0:
            term = lax.dot_general(
                tile[index * band : (index + 1) * band, :],
                tile[0:width, :],
                (((1,), (1,)), ((), ())),
                preferred_element_type=F32,
            )
        else:
            term = lax.dot_general(
                tile[:, index * band : (index + 1) * band],
                tile[:, 0:width],
                (((0,), (0,)), ((), ())),
                preferred_element_type=F32,
            )
        place = (slice(row, row + band), slice(col, col + width))
        part[place] = term if first else part[place] + term
    place = (slice(5 * band, 5 * band + order), slice(0, order))
    term = tile[...].astype(F32)
    part[place] = term if first else part[place] + term


def sum_kernel(
    trials_n, data_n, chunks, grads, total, mine, part, swap, passed, outgoing,
    grad_send, grad_recv, swap_send, swap_recv, pass_send, pass_recv,
    back_send, back_recv, share_send, share_recv,
):
    here_t = lax.axis_index("trial")
    here_d = lax.axis_index("dp")
    chips = data_n // 2
    core = lax.rem(here_d, 2)
    chip = here_d // 2
    partner = here_d + 1 - 2 * core
    rows = part.shape[0]
    half = rows // 2
    size = half // (2 * chunks)

    barrier = pltpu.get_barrier_semaphore()
    for step in range(1, trials_n):
        peer = lax.rem(here_t + step, trials_n)
        pl.semaphore_signal(barrier, inc=1, device_id=(peer, here_d), device_id_type=MESH)
    pl.semaphore_signal(barrier, inc=1, device_id=(here_t, partner), device_id_type=MESH)

    @pl.when(chip > 0)
    def _():
        pl.semaphore_signal(barrier, inc=1, device_id=(here_t, here_d - 2), device_id_type=MESH)

    @pl.when(chip < chips - 1)
    def _():
        pl.semaphore_signal(barrier, inc=1, device_id=(here_t, here_d + 2), device_id_type=MESH)

    neighbours = jnp.where(chip > 0, 1, 0) + jnp.where(chip < chips - 1, 1, 0)
    pl.semaphore_wait(barrier, trials_n + neighbours)

    def grad_copy(step):
        peer = lax.rem(here_t + step, trials_n)
        return pltpu.make_async_remote_copy(
            src_ref=grads.at[peer],
            dst_ref=mine.at[step - 1],
            send_sem=grad_send.at[step - 1],
            recv_sem=grad_recv.at[step - 1],
            device_id=(peer, here_d),
            device_id_type=MESH,
        )

    for step in range(1, trials_n):
        grad_copy(step).start()
    add_tile(part, grads.at[here_t], True)
    for step in range(1, trials_n):
        grad_copy(step).wait_recv()
        add_tile(part, mine.at[step - 1], False)

    def chunk_at(owner, way, k):
        return pl.ds(pl.multiple_of(owner * half + (way * chunks + k) * size, 8), size)

    def swap_copy(way, k):
        return pltpu.make_async_remote_copy(
            src_ref=part.at[chunk_at(1 - core, way, k)],
            dst_ref=swap.at[way, k],
            send_sem=swap_send.at[way, k],
            recv_sem=swap_recv.at[way, k],
            device_id=(here_t, partner),
            device_id_type=MESH,
        )

    def pass_copy(way, k):
        return pltpu.make_async_remote_copy(
            src_ref=outgoing.at[way, k],
            dst_ref=passed.at[way, k],
            send_sem=pass_send.at[way, k],
            recv_sem=pass_recv.at[way, k],
            device_id=(here_t, here_d + 2 - 4 * way),
            device_id_type=MESH,
        )

    def back_copy(way, k):
        return pltpu.make_async_remote_copy(
            src_ref=total.at[chunk_at(core, way, k)],
            dst_ref=total.at[chunk_at(core, way, k)],
            send_sem=back_send.at[way, k],
            recv_sem=back_recv.at[way, k],
            device_id=(here_t, here_d - 2 + 4 * way),
            device_id_type=MESH,
        )

    def share_copy(way, k):
        return pltpu.make_async_remote_copy(
            src_ref=total.at[chunk_at(core, way, k)],
            dst_ref=total.at[chunk_at(core, way, k)],
            send_sem=share_send.at[way, k],
            recv_sem=share_recv.at[way, k],
            device_id=(here_t, partner),
            device_id_type=MESH,
        )

    def shared_by_partner(way, k):
        return pltpu.make_async_remote_copy(
            src_ref=total.at[chunk_at(1 - core, way, k)],
            dst_ref=total.at[chunk_at(1 - core, way, k)],
            send_sem=share_send.at[way, k],
            recv_sem=share_recv.at[way, k],
            device_id=(here_t, partner),
            device_id_type=MESH,
        )

    order = [(way, k) for k in range(chunks) for way in range(2)]
    is_start = (chip == 0, chip == chips - 1)
    is_end = (chip == chips - 1, chip == 0)

    for way, k in order:
        swap_copy(way, k).start()
    for way, k in order:
        swap_copy(way, k).wait_recv()
        outgoing[way, k] = part[chunk_at(core, way, k), :] + swap[way, k]

        @pl.when(jnp.logical_not(is_start[way]))
        def _():
            pass_copy(way, k).wait_recv()
            outgoing[way, k] = outgoing[way, k] + passed[way, k]

        @pl.when(jnp.logical_not(is_end[way]))
        def _():
            pass_copy(way, k).start()

        @pl.when(is_end[way])
        def _():
            total[chunk_at(core, way, k), :] = outgoing[way, k]
            back_copy(way, k).start()
            share_copy(way, k).start()

    for way, k in order:

        @pl.when(jnp.logical_not(is_end[way]))
        def _():
            back_copy(way, k).wait_recv()

            @pl.when(jnp.logical_not(is_start[way]))
            def _():
                back_copy(way, k).start()

            share_copy(way, k).start()

    for way, k in order:
        shared_by_partner(way, k).wait_recv()
    for way, k in order:
        swap_copy(way, k).wait_send()
        share_copy(way, k).wait_send()

        @pl.when(jnp.logical_not(is_end[way]))
        def _():
            pass_copy(way, k).wait_send()

        @pl.when(jnp.logical_not(is_start[way]))
        def _():
            back_copy(way, k).wait_send()

    for step in range(1, trials_n):
        grad_copy(step).wait_send()


def split(value):
    high = value.astype(BF16)
    return high, (value - high.astype(F32)).astype(BF16)


def product(first, second):
    def dot(a, b):
        return jnp.dot(a, b, preferred_element_type=F32)

    return dot(first[0], second[0]) + (dot(first[0], second[1]) + dot(first[1], second[0]))


def update_kernel(
    trials_n, data_n, settings, packed, exponents, dampings, out,
    stat, factor, square, cube, root_high, root_low, finished, own_sem, send_sem, recv_sem,
):
    here_t = lax.axis_index("trial")
    here_d = lax.axis_index("dp")
    devices = trials_n * data_n
    here = here_t * data_n + here_d
    order = packed.shape[1]
    setting = lax.rem(here_d, settings)

    barrier = pltpu.get_barrier_semaphore()

    @pl.loop(1, devices)
    def _(step):
        peer = lax.rem(here + step, devices)
        pl.semaphore_signal(
            barrier, inc=1, device_id=(peer // data_n, lax.rem(peer, data_n)), device_id_type=MESH
        )

    band, pieces = stat_pieces(order)
    exponent = jnp.full((1, 1), exponents[setting], jnp.int32)
    damping = jnp.full((1, 1), dampings[setting], F32)
    order_f = exponent.astype(F32)
    eye = (
        lax.broadcasted_iota(jnp.int32, (order, order), 0)
        == lax.broadcasted_iota(jnp.int32, (order, order), 1)
    )
    weight = 1.0 / (devices * order)

    for kind in range(2):
        for piece_kind, index, row, col in pieces:
            if piece_kind != kind:
                continue
            for other in range(index + 1):
                block = packed[row : row + band, col + other * band : col + (other + 1) * band]
                block = block * weight
                stat[index * band : (index + 1) * band, other * band : (other + 1) * band] = block
                if other < index:
                    stat[other * band : (other + 1) * band, index * band : (index + 1) * band] = (
                        block.T
                    )
        shifted = stat[...] + jnp.where(eye, damping, 0.0)
        norm = jnp.sqrt(jnp.sum(shifted * shifted, keepdims=True) + 1e-06)
        scaling = (1.0 + order_f) / (2.0 * norm)
        factor[...] = (jnp.where(eye, order_f + 1.0, 0.0) - scaling * shifted) / order_f
        factor_parts = split(factor[...])
        square[...] = product(factor_parts, factor_parts)
        square_parts = split(square[...])
        cube[...] = product(square_parts, factor_parts)
        low = jnp.where(exponent == 2, factor[...], square[...])
        high = jnp.where(exponent == 2, square[...], cube[...])
        outer = jnp.where(exponent == 4, cube[...], square[...])
        tail = product(split(outer), split(order_f * high - (order_f + 1.0) * low))
        root = (jnp.exp(jnp.log(scaling) / order_f) / order_f) * (
            (order_f + 1.0) * factor[...] + tail
        )
        root_high[kind], root_low[kind] = split(root)

    average = packed[5 * band : 5 * band + order, :] * (1.0 / devices)
    middle = product((root_high[0], root_low[0]), split(average))
    raw = product(split(middle), (root_high[1], root_low[1]))
    count = order * order
    target = jnp.sqrt(jnp.sum(average * average, keepdims=True) / count)
    spread = jnp.sqrt(jnp.sum(raw * raw, keepdims=True) / count + 1e-06)
    stat[...] = raw * target / spread
    row_share, col_share = out.shape[2:]
    for t in range(trials_n):
        for d in range(data_n):
            finished[t, d] = stat[
                d * row_share : (d + 1) * row_share, t * col_share : (t + 1) * col_share
            ].astype(BF16)

    pl.semaphore_wait(barrier, devices - 1)

    def block_copy(peer):
        peer_t, peer_d = peer // data_n, lax.rem(peer, data_n)
        return pltpu.make_async_remote_copy(
            src_ref=finished.at[peer_t, peer_d],
            dst_ref=out.at[here_d, here_t],
            send_sem=send_sem.at[peer],
            recv_sem=recv_sem.at[here_d, here_t],
            device_id=(peer_t, peer_d),
            device_id_type=MESH,
        )

    own = pltpu.make_async_copy(finished.at[here_t, here_d], out.at[setting, here_t], own_sem)

    @pl.when(here_d < settings)
    def _():
        own.start()

        @pl.loop(1, devices)
        def _(step):
            block_copy(lax.rem(here + step, devices)).start()

    @pl.loop(0, settings * trials_n)
    def _(source):
        source_t, source_d = source // settings, lax.rem(source, settings)

        @pl.when(source_t * data_n + source_d != here)
        def _():
            pltpu.make_async_remote_copy(
                src_ref=finished.at[here_t, here_d],
                dst_ref=out.at[source_d, source_t],
                send_sem=send_sem.at[here],
                recv_sem=recv_sem.at[source_d, source_t],
                device_id=(source_t, source_d),
                device_id_type=MESH,
            ).wait_recv()

    @pl.when(here_d < settings)
    def _():
        own.wait()

        @pl.loop(1, devices)
        def _(step):
            block_copy(lax.rem(here + step, devices)).wait_send()


def per_device(grads, exponents, dampings):
    trials_n = lax.axis_size("trial")
    data_n = lax.axis_size("dp")
    devices = trials_n * data_n
    settings = exponents.shape[0]
    tiles, order = grads.shape[1], grads.shape[-1]
    assert tiles == trials_n and data_n >= settings and data_n % 2 == 0
    rows = packed_rows(order)
    size = rows // (4 * CHUNKS)
    in_vmem = pl.BlockSpec(memory_space=pltpu.VMEM)
    in_smem = pl.BlockSpec(memory_space=pltpu.SMEM)
    dma = pltpu.SemaphoreType.DMA
    pairs = dma((2, CHUNKS))

    packed = pl.pallas_call(
        functools.partial(sum_kernel, trials_n, data_n, CHUNKS),
        out_shape=jax.ShapeDtypeStruct((rows, order), F32),
        in_specs=[in_vmem],
        out_specs=in_vmem,
        scratch_shapes=[
            pltpu.VMEM((trials_n - 1, order, order), BF16),
            pltpu.VMEM((rows, order), F32),
            pltpu.VMEM((2, CHUNKS, size, order), F32),
            pltpu.VMEM((2, CHUNKS, size, order), F32),
            pltpu.VMEM((2, CHUNKS, size, order), F32),
            dma((trials_n - 1,)),
            dma((trials_n - 1,)),
        ]
        + [pairs] * 8,
        compiler_params=pltpu.CompilerParams(
            collective_id=0, has_side_effects=True, vmem_limit_bytes=40 * 1024 * 1024
        ),
    )(grads[0])

    out = pl.pallas_call(
        functools.partial(update_kernel, trials_n, data_n, settings),
        out_shape=jax.ShapeDtypeStruct(
            (settings, tiles, order // data_n, order // trials_n), BF16
        ),
        in_specs=[in_vmem, in_smem, in_smem],
        out_specs=in_vmem,
        scratch_shapes=[
            pltpu.VMEM((order, order), F32),
            pltpu.VMEM((order, order), F32),
            pltpu.VMEM((order, order), F32),
            pltpu.VMEM((order, order), F32),
            pltpu.VMEM((2, order, order), BF16),
            pltpu.VMEM((2, order, order), BF16),
            pltpu.VMEM((trials_n, data_n, order // data_n, order // trials_n), BF16),
            dma,
            dma((devices,)),
            dma((settings, trials_n)),
        ],
        compiler_params=pltpu.CompilerParams(
            collective_id=1, has_side_effects=True, vmem_limit_bytes=40 * 1024 * 1024
        ),
    )(packed, exponents, dampings)
    return out


def solution(mesh):
    placed = (P(("trial", "dp"), None, None, None), P(), P())
    return jax.shard_map(
        per_device,
        mesh=mesh,
        in_specs=placed,
        out_specs=P(None, None, "dp", "trial"),
        check_vma=False,
    )
```

```python
import functools

import jax
import jax.numpy as jnp
from jax import lax
from jax.experimental import pallas as pl
from jax.experimental.pallas import tpu as pltpu
from jax.sharding import PartitionSpec as P

MESH = pl.DeviceIdType.MESH
BANDS = 4
CHUNKS = 3
F32 = jnp.float32
BF16 = jnp.bfloat16


def stat_pieces(order):
    band = order // BANDS
    pieces = []
    for kind in range(2):
        base = kind * 2 * band
        pieces.append((kind, 3, base, 0))
        pieces.append((kind, 2, base + band, 0))
        pieces.append((kind, 0, base + band, 3 * band))
        pieces.append((kind, 1, 4 * band, kind * 2 * band))
    return band, pieces


def packed_rows(order):
    return 5 * (order // BANDS) + order


def add_tile(part, tile, first):
    order = part.shape[1]
    band, pieces = stat_pieces(order)
    for kind, index, row, col in pieces:
        width = (index + 1) * band
        if kind == 0:
            term = lax.dot_general(
                tile[index * band : (index + 1) * band, :],
                tile[0:width, :],
                (((1,), (1,)), ((), ())),
                preferred_element_type=F32,
            )
        else:
            term = lax.dot_general(
                tile[:, index * band : (index + 1) * band],
                tile[:, 0:width],
                (((0,), (0,)), ((), ())),
                preferred_element_type=F32,
            )
        place = (slice(row, row + band), slice(col, col + width))
        part[place] = term if first else part[place] + term
    place = (slice(5 * band, 5 * band + order), slice(0, order))
    term = tile[...].astype(F32)
    part[place] = term if first else part[place] + term


def sum_kernel(
    trials_n, data_n, chunks, grads, total, mine, part, swap, passed, outgoing,
    grad_send, grad_recv, swap_send, swap_recv, pass_send, pass_recv,
    back_send, back_recv, share_send, share_recv,
):
    here_t = lax.axis_index("trial")
    here_d = lax.axis_index("dp")
    chips = data_n // 2
    core = lax.rem(here_d, 2)
    chip = here_d // 2
    partner = here_d + 1 - 2 * core
    rows = part.shape[0]
    half = rows // 2
    size = half // (2 * chunks)

    barrier = pltpu.get_barrier_semaphore()
    for step in range(1, trials_n):
        peer = lax.rem(here_t + step, trials_n)
        pl.semaphore_signal(barrier, inc=1, device_id=(peer, here_d), device_id_type=MESH)
    pl.semaphore_signal(barrier, inc=1, device_id=(here_t, partner), device_id_type=MESH)

    @pl.when(chip > 0)
    def _():
        pl.semaphore_signal(barrier, inc=1, device_id=(here_t, here_d - 2), device_id_type=MESH)

    @pl.when(chip < chips - 1)
    def _():
        pl.semaphore_signal(barrier, inc=1, device_id=(here_t, here_d + 2), device_id_type=MESH)

    neighbours = jnp.where(chip > 0, 1, 0) + jnp.where(chip < chips - 1, 1, 0)
    pl.semaphore_wait(barrier, trials_n + neighbours)

    def grad_copy(step):
        peer = lax.rem(here_t + step, trials_n)
        return pltpu.make_async_remote_copy(
            src_ref=grads.at[peer],
            dst_ref=mine.at[step - 1],
            send_sem=grad_send.at[step - 1],
            recv_sem=grad_recv.at[step - 1],
            device_id=(peer, here_d),
            device_id_type=MESH,
        )

    for step in range(1, trials_n):
        grad_copy(step).start()
    add_tile(part, grads.at[here_t], True)
    for step in range(1, trials_n):
        grad_copy(step).wait_recv()
        add_tile(part, mine.at[step - 1], False)

    def chunk_at(owner, way, k):
        return pl.ds(pl.multiple_of(owner * half + (way * chunks + k) * size, 8), size)

    def swap_copy(way, k):
        return pltpu.make_async_remote_copy(
            src_ref=part.at[chunk_at(1 - core, way, k)],
            dst_ref=swap.at[way, k],
            send_sem=swap_send.at[way, k],
            recv_sem=swap_recv.at[way, k],
            device_id=(here_t, partner),
            device_id_type=MESH,
        )

    def pass_copy(way, k):
        return pltpu.make_async_remote_copy(
            src_ref=outgoing.at[way, k],
            dst_ref=passed.at[way, k],
            send_sem=pass_send.at[way, k],
            recv_sem=pass_recv.at[way, k],
            device_id=(here_t, here_d + 2 - 4 * way),
            device_id_type=MESH,
        )

    def back_copy(way, k):
        return pltpu.make_async_remote_copy(
            src_ref=total.at[chunk_at(core, way, k)],
            dst_ref=total.at[chunk_at(core, way, k)],
            send_sem=back_send.at[way, k],
            recv_sem=back_recv.at[way, k],
            device_id=(here_t, here_d - 2 + 4 * way),
            device_id_type=MESH,
        )

    def share_copy(way, k):
        return pltpu.make_async_remote_copy(
            src_ref=total.at[chunk_at(core, way, k)],
            dst_ref=total.at[chunk_at(core, way, k)],
            send_sem=share_send.at[way, k],
            recv_sem=share_recv.at[way, k],
            device_id=(here_t, partner),
            device_id_type=MESH,
        )

    def shared_by_partner(way, k):
        return pltpu.make_async_remote_copy(
            src_ref=total.at[chunk_at(1 - core, way, k)],
            dst_ref=total.at[chunk_at(1 - core, way, k)],
            send_sem=share_send.at[way, k],
            recv_sem=share_recv.at[way, k],
            device_id=(here_t, partner),
            device_id_type=MESH,
        )

    order = [(way, k) for k in range(chunks) for way in range(2)]
    is_start = (chip == 0, chip == chips - 1)
    is_end = (chip == chips - 1, chip == 0)

    for way, k in order:
        swap_copy(way, k).start()
    last = chips - 1
    distance = (chip, last - chip)

    def reduce_chunk(way, k):
        swap_copy(way, k).wait_recv()
        outgoing[way, k] = part[chunk_at(core, way, k), :] + swap[way, k]

        @pl.when(jnp.logical_not(is_start[way]))
        def _():
            pass_copy(way, k).wait_recv()
            outgoing[way, k] = outgoing[way, k] + passed[way, k]

        @pl.when(jnp.logical_not(is_end[way]))
        def _():
            pass_copy(way, k).start()

        @pl.when(is_end[way])
        def _():
            total[chunk_at(core, way, k), :] = outgoing[way, k]
            back_copy(way, k).start()
            share_copy(way, k).start()

    def return_chunk(way, k):
        back_copy(way, k).wait_recv()

        @pl.when(jnp.logical_not(is_start[way]))
        def _():
            back_copy(way, k).start()

        share_copy(way, k).start()

    @pl.loop(0, chunks + 2 * last)
    def _(step):
        for way in range(2):
            k = step - distance[way]

            @pl.when((k >= 0) & (k < chunks))
            def _():
                reduce_chunk(way, k)

        for way in range(2):
            k = step - last - distance[1 - way]

            @pl.when((k >= 0) & (k < chunks) & jnp.logical_not(is_end[way]))
            def _():
                return_chunk(way, k)

    for way, k in order:
        shared_by_partner(way, k).wait_recv()
    for way, k in order:
        swap_copy(way, k).wait_send()
        share_copy(way, k).wait_send()

        @pl.when(jnp.logical_not(is_end[way]))
        def _():
            pass_copy(way, k).wait_send()

        @pl.when(jnp.logical_not(is_start[way]))
        def _():
            back_copy(way, k).wait_send()

    for step in range(1, trials_n):
        grad_copy(step).wait_send()


def split(value):
    high = value.astype(BF16)
    return high, (value - high.astype(F32)).astype(BF16)


def product(first, second):
    def dot(a, b):
        return jnp.dot(a, b, preferred_element_type=F32)

    return dot(first[0], second[0]) + (dot(first[0], second[1]) + dot(first[1], second[0]))


def update_kernel(
    trials_n, data_n, settings, packed, exponents, dampings, out,
    stat, factor, square, cube, root_high, root_low, finished, own_sem, send_sem, recv_sem,
):
    here_t = lax.axis_index("trial")
    here_d = lax.axis_index("dp")
    devices = trials_n * data_n
    here = here_t * data_n + here_d
    order = packed.shape[1]
    setting = lax.rem(here_d, settings)

    barrier = pltpu.get_barrier_semaphore()

    @pl.loop(1, devices)
    def _(step):
        peer = lax.rem(here + step, devices)
        pl.semaphore_signal(
            barrier, inc=1, device_id=(peer // data_n, lax.rem(peer, data_n)), device_id_type=MESH
        )

    band, pieces = stat_pieces(order)
    exponent = jnp.full((1, 1), exponents[setting], jnp.int32)
    damping = jnp.full((1, 1), dampings[setting], F32)
    order_f = exponent.astype(F32)
    eye = (
        lax.broadcasted_iota(jnp.int32, (order, order), 0)
        == lax.broadcasted_iota(jnp.int32, (order, order), 1)
    )
    weight = 1.0 / (devices * order)

    for kind in range(2):
        for piece_kind, index, row, col in pieces:
            if piece_kind != kind:
                continue
            for other in range(index + 1):
                block = packed[row : row + band, col + other * band : col + (other + 1) * band]
                block = block * weight
                stat[index * band : (index + 1) * band, other * band : (other + 1) * band] = block
                if other < index:
                    stat[other * band : (other + 1) * band, index * band : (index + 1) * band] = (
                        block.T
                    )
        shifted = stat[...] + jnp.where(eye, damping, 0.0)
        norm = jnp.sqrt(jnp.sum(shifted * shifted, keepdims=True) + 1e-06)
        scaling = (1.0 + order_f) / (2.0 * norm)
        factor[...] = (jnp.where(eye, order_f + 1.0, 0.0) - scaling * shifted) / order_f
        factor_parts = split(factor[...])
        square[...] = product(factor_parts, factor_parts)
        square_parts = split(square[...])
        cube[...] = product(square_parts, factor_parts)
        low = jnp.where(exponent == 2, factor[...], square[...])
        high = jnp.where(exponent == 2, square[...], cube[...])
        outer = jnp.where(exponent == 4, cube[...], square[...])
        tail = product(split(outer), split(order_f * high - (order_f + 1.0) * low))
        root = (jnp.exp(jnp.log(scaling) / order_f) / order_f) * (
            (order_f + 1.0) * factor[...] + tail
        )
        root_high[kind], root_low[kind] = split(root)

    average = packed[5 * band : 5 * band + order, :] * (1.0 / devices)
    middle = product((root_high[0], root_low[0]), split(average))
    raw = product(split(middle), (root_high[1], root_low[1]))
    count = order * order
    target = jnp.sqrt(jnp.sum(average * average, keepdims=True) / count)
    spread = jnp.sqrt(jnp.sum(raw * raw, keepdims=True) / count + 1e-06)
    stat[...] = raw * target / spread
    row_share, col_share = out.shape[2:]
    for t in range(trials_n):
        for d in range(data_n):
            finished[t, d] = stat[
                d * row_share : (d + 1) * row_share, t * col_share : (t + 1) * col_share
            ].astype(BF16)

    pl.semaphore_wait(barrier, devices - 1)

    def block_copy(peer):
        peer_t, peer_d = peer // data_n, lax.rem(peer, data_n)
        return pltpu.make_async_remote_copy(
            src_ref=finished.at[peer_t, peer_d],
            dst_ref=out.at[here_d, here_t],
            send_sem=send_sem.at[peer],
            recv_sem=recv_sem.at[here_d, here_t],
            device_id=(peer_t, peer_d),
            device_id_type=MESH,
        )

    own = pltpu.make_async_copy(finished.at[here_t, here_d], out.at[setting, here_t], own_sem)

    @pl.when(here_d < settings)
    def _():
        own.start()

        @pl.loop(1, devices)
        def _(step):
            block_copy(lax.rem(here + step, devices)).start()

    @pl.loop(0, settings * trials_n)
    def _(source):
        source_t, source_d = source // settings, lax.rem(source, settings)

        @pl.when(source_t * data_n + source_d != here)
        def _():
            pltpu.make_async_remote_copy(
                src_ref=finished.at[here_t, here_d],
                dst_ref=out.at[source_d, source_t],
                send_sem=send_sem.at[here],
                recv_sem=recv_sem.at[source_d, source_t],
                device_id=(source_t, source_d),
                device_id_type=MESH,
            ).wait_recv()

    @pl.when(here_d < settings)
    def _():
        own.wait()

        @pl.loop(1, devices)
        def _(step):
            block_copy(lax.rem(here + step, devices)).wait_send()


def per_device(grads, exponents, dampings):
    trials_n = lax.axis_size("trial")
    data_n = lax.axis_size("dp")
    devices = trials_n * data_n
    settings = exponents.shape[0]
    tiles, order = grads.shape[1], grads.shape[-1]
    assert tiles == trials_n and data_n >= settings and data_n % 2 == 0
    rows = packed_rows(order)
    size = rows // (4 * CHUNKS)
    in_vmem = pl.BlockSpec(memory_space=pltpu.VMEM)
    in_smem = pl.BlockSpec(memory_space=pltpu.SMEM)
    dma = pltpu.SemaphoreType.DMA
    pairs = dma((2, CHUNKS))

    packed = pl.pallas_call(
        functools.partial(sum_kernel, trials_n, data_n, CHUNKS),
        out_shape=jax.ShapeDtypeStruct((rows, order), F32),
        in_specs=[in_vmem],
        out_specs=in_vmem,
        scratch_shapes=[
            pltpu.VMEM((trials_n - 1, order, order), BF16),
            pltpu.VMEM((rows, order), F32),
            pltpu.VMEM((2, CHUNKS, size, order), F32),
            pltpu.VMEM((2, CHUNKS, size, order), F32),
            pltpu.VMEM((2, CHUNKS, size, order), F32),
            dma((trials_n - 1,)),
            dma((trials_n - 1,)),
        ]
        + [pairs] * 8,
        compiler_params=pltpu.CompilerParams(
            collective_id=0, has_side_effects=True, vmem_limit_bytes=40 * 1024 * 1024
        ),
    )(grads[0])

    out = pl.pallas_call(
        functools.partial(update_kernel, trials_n, data_n, settings),
        out_shape=jax.ShapeDtypeStruct(
            (settings, tiles, order // data_n, order // trials_n), BF16
        ),
        in_specs=[in_vmem, in_smem, in_smem],
        out_specs=in_vmem,
        scratch_shapes=[
            pltpu.VMEM((order, order), F32),
            pltpu.VMEM((order, order), F32),
            pltpu.VMEM((order, order), F32),
            pltpu.VMEM((order, order), F32),
            pltpu.VMEM((2, order, order), BF16),
            pltpu.VMEM((2, order, order), BF16),
            pltpu.VMEM((trials_n, data_n, order // data_n, order // trials_n), BF16),
            dma,
            dma((devices,)),
            dma((settings, trials_n)),
        ],
        compiler_params=pltpu.CompilerParams(
            collective_id=1, has_side_effects=True, vmem_limit_bytes=40 * 1024 * 1024
        ),
    )(packed, exponents, dampings)
    return out


def solution(mesh):
    placed = (P(("trial", "dp"), None, None, None), P(), P())
    return jax.shard_map(
        per_device,
        mesh=mesh,
        in_specs=placed,
        out_specs=P(None, None, "dp", "trial"),
        check_vma=False,
    )
```

```python
import functools

import jax
import jax.numpy as jnp
from jax import lax
from jax.experimental import pallas as pl
from jax.experimental.pallas import tpu as pltpu
from jax.sharding import PartitionSpec as P

MESH = pl.DeviceIdType.MESH
BANDS = 4
F32 = jnp.float32
BF16 = jnp.bfloat16


def stat_pieces(order):
    band = order // BANDS
    places = {
        (0, 2): (3, 0),
        (0, 0): (3, 3),
        (0, 3): (5, 0),
        (0, 1): (6, 0),
        (1, 1): (6, 2),
        (1, 2): (7, 0),
        (1, 0): (7, 3),
        (1, 3): (8, 0),
    }
    return band, {key: (row * band, col * band) for key, (row, col) in places.items()}


MEAN_BANDS = (0, 1, 2, 4)
READY = ((0,), (1,), (2, 3), (4, 5, 6, 7, 8))
PACKED_BANDS = 9


def add_band(part, tiles, index):
    order = part.shape[1]
    band, pieces = stat_pieces(order)
    rows = slice(index * band, (index + 1) * band)

    def store(key, terms):
        row, col = pieces[key]
        total = sum(terms[1:], terms[0])
        part[row : row + band, col : col + total.shape[1]] = total

    mean = [tile[rows, :].astype(F32) for tile in tiles]
    start = MEAN_BANDS[index] * band
    part[start : start + band, :] = sum(mean[1:], mean[0])
    width = (index + 1) * band
    store(
        (0, index),
        [
            lax.dot_general(
                tile[rows, :], tile[0:width, :], (((1,), (1,)), ((), ())),
                preferred_element_type=F32,
            )
            for tile in tiles
        ],
    )
    if index < BANDS - 1:
        return
    for other in range(BANDS):
        width = (other + 1) * band
        store(
            (1, other),
            [
                lax.dot_general(
                    tile[:, other * band : width], tile[:, 0:width], (((0,), (0,)), ((), ())),
                    preferred_element_type=F32,
                )
                for tile in tiles
            ],
        )


def sum_kernel(
    trials_n, data_n, chunks, grads, total, mine, part, swap, passed, outgoing,
    grad_send, grad_recv, swap_send, swap_recv, pass_send, pass_recv,
    back_send, back_recv, share_send, share_recv,
):
    here_t = lax.axis_index("trial")
    here_d = lax.axis_index("dp")
    chips = data_n // 2
    core = lax.rem(here_d, 2)
    chip = here_d // 2
    partner = here_d + 1 - 2 * core
    last = chips - 1
    band = part.shape[0] // chunks
    size = band // 4

    barrier = pltpu.get_barrier_semaphore()
    for step in range(1, trials_n):
        peer = lax.rem(here_t + step, trials_n)
        pl.semaphore_signal(barrier, inc=1, device_id=(peer, here_d), device_id_type=MESH)
    pl.semaphore_signal(barrier, inc=1, device_id=(here_t, partner), device_id_type=MESH)

    @pl.when(chip > 0)
    def _():
        pl.semaphore_signal(barrier, inc=1, device_id=(here_t, here_d - 2), device_id_type=MESH)

    @pl.when(chip < chips - 1)
    def _():
        pl.semaphore_signal(barrier, inc=1, device_id=(here_t, here_d + 2), device_id_type=MESH)

    neighbours = jnp.where(chip > 0, 1, 0) + jnp.where(chip < chips - 1, 1, 0)
    pl.semaphore_wait(barrier, trials_n + neighbours)

    def grad_copy(step, index):
        peer = lax.rem(here_t + step, trials_n)
        band_rows = pl.ds(index * band, band)
        return pltpu.make_async_remote_copy(
            src_ref=grads.at[peer, band_rows],
            dst_ref=mine.at[step - 1, band_rows],
            send_sem=grad_send.at[step - 1, index],
            recv_sem=grad_recv.at[step - 1, index],
            device_id=(peer, here_d),
            device_id_type=MESH,
        )

    for index in range(BANDS):
        for step in range(1, trials_n):
            grad_copy(step, index).start()

    def chunk_at(owner, way, k):
        return pl.ds(pl.multiple_of(k * band + (owner * 2 + way) * size, 8), size)

    def swap_copy(way, k):
        return pltpu.make_async_remote_copy(
            src_ref=part.at[chunk_at(1 - core, way, k)],
            dst_ref=swap.at[way, k],
            send_sem=swap_send.at[way, k],
            recv_sem=swap_recv.at[way, k],
            device_id=(here_t, partner),
            device_id_type=MESH,
        )

    owner = (chips // 2, chips // 2 - 1)
    farthest = chips // 2

    def pass_copy(way, k):
        side = jnp.where(chip < owner[way], 0, 1)
        return pltpu.make_async_remote_copy(
            src_ref=outgoing.at[way, k],
            dst_ref=passed.at[way, side, k],
            send_sem=pass_send.at[way, k],
            recv_sem=pass_recv.at[way, side, k],
            device_id=(here_t, here_d + 2 - 4 * side),
            device_id_type=MESH,
        )

    def passed_from(way, side, k):
        return pltpu.make_async_remote_copy(
            src_ref=outgoing.at[way, k],
            dst_ref=passed.at[way, side, k],
            send_sem=pass_send.at[way, k],
            recv_sem=pass_recv.at[way, side, k],
            device_id=(here_t, here_d - 2 + 4 * side),
            device_id_type=MESH,
        )

    def back_copy(way, side, k):
        return pltpu.make_async_remote_copy(
            src_ref=total.at[chunk_at(core, way, k)],
            dst_ref=total.at[chunk_at(core, way, k)],
            send_sem=back_send.at[way, side, k],
            recv_sem=back_recv.at[way, k],
            device_id=(here_t, here_d - 2 + 4 * side),
            device_id_type=MESH,
        )

    def share_copy(way, k):
        return pltpu.make_async_remote_copy(
            src_ref=total.at[chunk_at(core, way, k)],
            dst_ref=total.at[chunk_at(core, way, k)],
            send_sem=share_send.at[way, k],
            recv_sem=share_recv.at[way, k],
            device_id=(here_t, partner),
            device_id_type=MESH,
        )

    def shared_by_partner(way, k):
        return pltpu.make_async_remote_copy(
            src_ref=total.at[chunk_at(1 - core, way, k)],
            dst_ref=total.at[chunk_at(1 - core, way, k)],
            send_sem=share_send.at[way, k],
            recv_sem=share_recv.at[way, k],
            device_id=(here_t, partner),
            device_id_type=MESH,
        )

    def sends_back(way):
        return (
            (chip <= owner[way]) & (chip > 0),
            (chip >= owner[way]) & (chip < last),
        )

    def send_back(way, k):
        for side in range(2):

            @pl.when(sends_back(way)[side])
            def _():
                back_copy(way, side, k).start()

        share_copy(way, k).start()

    def reduce_chunk(way, k):
        swap_copy(way, k).wait_recv()
        outgoing[way, k] = part[chunk_at(core, way, k), :] + swap[way, k]
        arrives = ((chip > 0) & (chip <= owner[way]), (chip < last) & (chip >= owner[way]))
        for side in range(2):

            @pl.when(arrives[side])
            def _():
                passed_from(way, side, k).wait_recv()
                outgoing[way, k] = outgoing[way, k] + passed[way, side, k]

        @pl.when(chip != owner[way])
        def _():
            pass_copy(way, k).start()

        @pl.when(chip == owner[way])
        def _():
            total[chunk_at(core, way, k), :] = outgoing[way, k]
            send_back(way, k)

    def return_chunk(way, k):
        back_copy(way, 0, k).wait_recv()
        send_back(way, k)

    def chain_step(step):
        for way in range(2):
            hops = jnp.where(
                chip < owner[way], chip, jnp.where(chip > owner[way], last - chip, farthest)
            )
            k = step - hops

            @pl.when((k >= 0) & (k < chunks))
            def _():
                reduce_chunk(way, k)

        for way in range(2):
            away = jnp.where(chip < owner[way], owner[way] - chip, chip - owner[way])
            k = step - farthest - away

            @pl.when((k >= 0) & (k < chunks) & (away > 0))
            def _():
                return_chunk(way, k)

    tiles = [grads.at[here_t]] + [mine.at[step] for step in range(trials_n - 1)]
    for index in range(BANDS):
        for step in range(1, trials_n):
            grad_copy(step, index).wait_recv()
        add_band(part, tiles, index)
        for k in READY[index]:
            for way in range(2):
                swap_copy(way, k).start()
        if index < BANDS - 1:
            for k in READY[index]:
                chain_step(k)

    @pl.loop(READY[-1][0], chunks + 2 * farthest)
    def _(step):
        chain_step(step)

    order = [(way, k) for k in range(chunks) for way in range(2)]
    for way, k in order:
        shared_by_partner(way, k).wait_recv()
    for way, k in order:
        swap_copy(way, k).wait_send()
        share_copy(way, k).wait_send()

        @pl.when(chip != owner[way])
        def _():
            pass_copy(way, k).wait_send()

        for side in range(2):

            @pl.when(sends_back(way)[side])
            def _():
                back_copy(way, side, k).wait_send()

    for index in range(BANDS):
        for step in range(1, trials_n):
            grad_copy(step, index).wait_send()


def split(value):
    high = value.astype(BF16)
    return high, (value - high.astype(F32)).astype(BF16)


def product(first, second):
    def dot(a, b):
        return jnp.dot(a, b, preferred_element_type=F32)

    return dot(first[0], second[0]) + (dot(first[0], second[1]) + dot(first[1], second[0]))


def update_kernel(
    trials_n, data_n, settings, packed, exponents, dampings, out,
    stat, factor, square, cube, root_high, root_low, finished, own_sem, send_sem, recv_sem,
):
    here_t = lax.axis_index("trial")
    here_d = lax.axis_index("dp")
    devices = trials_n * data_n
    here = here_t * data_n + here_d
    order = packed.shape[1]
    setting = lax.rem(here_d, settings)

    barrier = pltpu.get_barrier_semaphore()

    @pl.loop(1, devices)
    def _(step):
        peer = lax.rem(here + step, devices)
        pl.semaphore_signal(
            barrier, inc=1, device_id=(peer // data_n, lax.rem(peer, data_n)), device_id_type=MESH
        )

    band, pieces = stat_pieces(order)
    exponent = jnp.full((1, 1), exponents[setting], jnp.int32)
    damping = jnp.full((1, 1), dampings[setting], F32)
    order_f = exponent.astype(F32)
    eye = (
        lax.broadcasted_iota(jnp.int32, (order, order), 0)
        == lax.broadcasted_iota(jnp.int32, (order, order), 1)
    )
    weight = 1.0 / (devices * order)

    for kind in range(2):
        for index in range(BANDS):
            row, col = pieces[kind, index]
            for other in range(index + 1):
                block = packed[row : row + band, col + other * band : col + (other + 1) * band]
                block = block * weight
                stat[index * band : (index + 1) * band, other * band : (other + 1) * band] = block
                if other < index:
                    stat[other * band : (other + 1) * band, index * band : (index + 1) * band] = (
                        block.T
                    )
        shifted = stat[...] + jnp.where(eye, damping, 0.0)
        norm = jnp.sqrt(jnp.sum(shifted * shifted, keepdims=True) + 1e-06)
        scaling = (1.0 + order_f) / (2.0 * norm)
        factor[...] = (jnp.where(eye, order_f + 1.0, 0.0) - scaling * shifted) / order_f
        factor_parts = split(factor[...])
        square[...] = product(factor_parts, factor_parts)
        square_parts = split(square[...])
        cube[...] = product(square_parts, factor_parts)
        low = jnp.where(exponent == 2, factor[...], square[...])
        high = jnp.where(exponent == 2, square[...], cube[...])
        outer = jnp.where(exponent == 4, cube[...], square[...])
        tail = product(split(outer), split(order_f * high - (order_f + 1.0) * low))
        root = (jnp.exp(jnp.log(scaling) / order_f) / order_f) * (
            (order_f + 1.0) * factor[...] + tail
        )
        root_high[kind], root_low[kind] = split(root)

    average = jnp.concatenate(
        [packed[row * band : (row + 1) * band, :] for row in MEAN_BANDS], axis=0
    ) * (1.0 / devices)
    middle = product((root_high[0], root_low[0]), split(average))
    raw = product(split(middle), (root_high[1], root_low[1]))
    count = order * order
    target = jnp.sqrt(jnp.sum(average * average, keepdims=True) / count)
    spread = jnp.sqrt(jnp.sum(raw * raw, keepdims=True) / count + 1e-06)
    stat[...] = raw * target / spread
    row_share, col_share = out.shape[2:]
    for t in range(trials_n):
        for d in range(data_n):
            finished[t, d] = stat[
                d * row_share : (d + 1) * row_share, t * col_share : (t + 1) * col_share
            ].astype(BF16)

    pl.semaphore_wait(barrier, devices - 1)

    def block_copy(peer):
        peer_t, peer_d = peer // data_n, lax.rem(peer, data_n)
        return pltpu.make_async_remote_copy(
            src_ref=finished.at[peer_t, peer_d],
            dst_ref=out.at[here_d, here_t],
            send_sem=send_sem.at[peer],
            recv_sem=recv_sem.at[here_d, here_t],
            device_id=(peer_t, peer_d),
            device_id_type=MESH,
        )

    own = pltpu.make_async_copy(finished.at[here_t, here_d], out.at[setting, here_t], own_sem)

    @pl.when(here_d < settings)
    def _():
        own.start()

        @pl.loop(1, devices)
        def _(step):
            block_copy(lax.rem(here + step, devices)).start()

    @pl.loop(0, settings * trials_n)
    def _(source):
        source_t, source_d = source // settings, lax.rem(source, settings)

        @pl.when(source_t * data_n + source_d != here)
        def _():
            pltpu.make_async_remote_copy(
                src_ref=finished.at[here_t, here_d],
                dst_ref=out.at[source_d, source_t],
                send_sem=send_sem.at[here],
                recv_sem=recv_sem.at[source_d, source_t],
                device_id=(source_t, source_d),
                device_id_type=MESH,
            ).wait_recv()

    @pl.when(here_d < settings)
    def _():
        own.wait()

        @pl.loop(1, devices)
        def _(step):
            block_copy(lax.rem(here + step, devices)).wait_send()


def per_device(grads, exponents, dampings):
    trials_n = lax.axis_size("trial")
    data_n = lax.axis_size("dp")
    devices = trials_n * data_n
    settings = exponents.shape[0]
    tiles, order = grads.shape[1], grads.shape[-1]
    assert tiles == trials_n and data_n >= settings and data_n % 2 == 0
    rows = PACKED_BANDS * (order // BANDS)
    size = order // BANDS // 4
    in_vmem = pl.BlockSpec(memory_space=pltpu.VMEM)
    in_smem = pl.BlockSpec(memory_space=pltpu.SMEM)
    dma = pltpu.SemaphoreType.DMA
    pairs = dma((2, PACKED_BANDS))
    sides = dma((2, 2, PACKED_BANDS))

    packed = pl.pallas_call(
        functools.partial(sum_kernel, trials_n, data_n, PACKED_BANDS),
        out_shape=jax.ShapeDtypeStruct((rows, order), F32),
        in_specs=[in_vmem],
        out_specs=in_vmem,
        scratch_shapes=[
            pltpu.VMEM((trials_n - 1, order, order), BF16),
            pltpu.VMEM((rows, order), F32),
            pltpu.VMEM((2, PACKED_BANDS, size, order), F32),
            pltpu.VMEM((2, 2, PACKED_BANDS, size, order), F32),
            pltpu.VMEM((2, PACKED_BANDS, size, order), F32),
            dma((trials_n - 1, BANDS)),
            dma((trials_n - 1, BANDS)),
            pairs,
            pairs,
            pairs,
            sides,
            sides,
            pairs,
            pairs,
            pairs,
        ],
        compiler_params=pltpu.CompilerParams(
            collective_id=0, has_side_effects=True, vmem_limit_bytes=40 * 1024 * 1024
        ),
    )(grads[0])

    out = pl.pallas_call(
        functools.partial(update_kernel, trials_n, data_n, settings),
        out_shape=jax.ShapeDtypeStruct(
            (settings, tiles, order // data_n, order // trials_n), BF16
        ),
        in_specs=[in_vmem, in_smem, in_smem],
        out_specs=in_vmem,
        scratch_shapes=[
            pltpu.VMEM((order, order), F32),
            pltpu.VMEM((order, order), F32),
            pltpu.VMEM((order, order), F32),
            pltpu.VMEM((order, order), F32),
            pltpu.VMEM((2, order, order), BF16),
            pltpu.VMEM((2, order, order), BF16),
            pltpu.VMEM((trials_n, data_n, order // data_n, order // trials_n), BF16),
            dma,
            dma((devices,)),
            dma((settings, trials_n)),
        ],
        compiler_params=pltpu.CompilerParams(
            collective_id=1, has_side_effects=True, vmem_limit_bytes=40 * 1024 * 1024
        ),
    )(packed, exponents, dampings)
    return out


def solution(mesh):
    placed = (P(("trial", "dp"), None, None, None), P(), P())
    return jax.shard_map(
        per_device,
        mesh=mesh,
        in_specs=placed,
        out_specs=P(None, None, "dp", "trial"),
        check_vma=False,
    )
```

```python
import functools

import jax
import jax.numpy as jnp
from jax import lax
from jax.experimental import pallas as pl
from jax.experimental.pallas import tpu as pltpu
from jax.sharding import PartitionSpec as P

MESH = pl.DeviceIdType.MESH
BANDS = 4
F32 = jnp.float32
BF16 = jnp.bfloat16


def stat_pieces(order):
    band = order // BANDS
    places = {
        (0, 2): (3, 0),
        (0, 0): (3, 3),
        (0, 3): (4, 0),
        (0, 1): (5, 0),
        (1, 1): (5, 2),
        (1, 2): (6, 0),
        (1, 0): (6, 3),
        (1, 3): (7, 0),
    }
    return band, {key: (row * band, col * band) for key, (row, col) in places.items()}


MEAN_BANDS = (0, 1, 2, 8)
STAT_ENDS = (5, 7)
READY = ((0,), (1,), (2, 3), (4, 5, 6, 7, 8))
PACKED_BANDS = 9


def add_band(part, tiles, index):
    order = part.shape[1]
    band, pieces = stat_pieces(order)
    rows = slice(index * band, (index + 1) * band)

    def store(key, terms):
        row, col = pieces[key]
        total = sum(terms[1:], terms[0])
        part[row : row + band, col : col + total.shape[1]] = total

    mean = [tile[rows, :].astype(F32) for tile in tiles]
    start = MEAN_BANDS[index] * band
    part[start : start + band, :] = sum(mean[1:], mean[0])
    width = (index + 1) * band
    store(
        (0, index),
        [
            lax.dot_general(
                tile[rows, :], tile[0:width, :], (((1,), (1,)), ((), ())),
                preferred_element_type=F32,
            )
            for tile in tiles
        ],
    )
    if index < BANDS - 1:
        return
    for other in range(BANDS):
        width = (other + 1) * band
        store(
            (1, other),
            [
                lax.dot_general(
                    tile[:, other * band : width], tile[:, 0:width], (((0,), (0,)), ((), ())),
                    preferred_element_type=F32,
                )
                for tile in tiles
            ],
        )


def split(value):
    high = value.astype(BF16)
    return high, (value - high.astype(F32)).astype(BF16)


def product(first, second):
    def dot(a, b):
        return jnp.dot(a, b, preferred_element_type=F32)

    return dot(first[0], second[0]) + (dot(first[0], second[1]) + dot(first[1], second[0]))


def update_kernel(
    trials_n, data_n, settings, chunks, grads, exponents, dampings, out,
    tile, mine, part, swap, passed, outgoing, total, stat, square, turned, root, finished,
    tile_sem, grad_send, grad_recv, swap_send, swap_recv, pass_send, pass_recv,
    back_send, back_recv, share_send, share_recv, own_sem, send_sem, recv_sem,
):
    here_t = lax.axis_index("trial")
    here_d = lax.axis_index("dp")
    devices = trials_n * data_n
    here = here_t * data_n + here_d
    setting = lax.rem(here_d, settings)
    chips = data_n // 2
    core = lax.rem(here_d, 2)
    chip = here_d // 2
    partner = here_d + 1 - 2 * core
    last = chips - 1
    band = part.shape[0] // chunks
    size = band // 4

    own_tile = pltpu.make_async_copy(grads.at[here_t], tile, tile_sem)
    own_tile.start()
    barrier = pltpu.get_barrier_semaphore()

    @pl.loop(1, devices)
    def _(step):
        peer = lax.rem(here + step, devices)
        pl.semaphore_signal(
            barrier, inc=1, device_id=(peer // data_n, lax.rem(peer, data_n)), device_id_type=MESH
        )

    pl.semaphore_wait(barrier, devices - 1)

    def grad_copy(step, index):
        peer = lax.rem(here_t + step, trials_n)
        band_rows = pl.ds(index * band, band)
        return pltpu.make_async_remote_copy(
            src_ref=grads.at[peer, band_rows],
            dst_ref=mine.at[step - 1, band_rows],
            send_sem=grad_send.at[step - 1, index],
            recv_sem=grad_recv.at[step - 1, index],
            device_id=(peer, here_d),
            device_id_type=MESH,
        )

    for index in range(BANDS):
        for step in range(1, trials_n):
            grad_copy(step, index).start()

    def chunk_at(owner, way, k):
        return pl.ds(pl.multiple_of(k * band + (owner * 2 + way) * size, 8), size)

    def swap_copy(way, k):
        return pltpu.make_async_remote_copy(
            src_ref=part.at[chunk_at(1 - core, way, k)],
            dst_ref=swap.at[way, k],
            send_sem=swap_send.at[way, k],
            recv_sem=swap_recv.at[way, k],
            device_id=(here_t, partner),
            device_id_type=MESH,
        )

    owner = (chips // 2, chips // 2 - 1)
    farthest = chips // 2

    def pass_copy(way, k):
        side = jnp.where(chip < owner[way], 0, 1)
        return pltpu.make_async_remote_copy(
            src_ref=outgoing.at[way, k],
            dst_ref=passed.at[way, side, k],
            send_sem=pass_send.at[way, k],
            recv_sem=pass_recv.at[way, side, k],
            device_id=(here_t, here_d + 2 - 4 * side),
            device_id_type=MESH,
        )

    def passed_from(way, side, k):
        return pltpu.make_async_remote_copy(
            src_ref=outgoing.at[way, k],
            dst_ref=passed.at[way, side, k],
            send_sem=pass_send.at[way, k],
            recv_sem=pass_recv.at[way, side, k],
            device_id=(here_t, here_d - 2 + 4 * side),
            device_id_type=MESH,
        )

    def back_copy(way, side, k):
        return pltpu.make_async_remote_copy(
            src_ref=total.at[chunk_at(core, way, k)],
            dst_ref=total.at[chunk_at(core, way, k)],
            send_sem=back_send.at[way, side, k],
            recv_sem=back_recv.at[way, k],
            device_id=(here_t, here_d - 2 + 4 * side),
            device_id_type=MESH,
        )

    def share_copy(way, k):
        return pltpu.make_async_remote_copy(
            src_ref=total.at[chunk_at(core, way, k)],
            dst_ref=total.at[chunk_at(core, way, k)],
            send_sem=share_send.at[way, k],
            recv_sem=share_recv.at[way, k],
            device_id=(here_t, partner),
            device_id_type=MESH,
        )

    def shared_by_partner(way, k):
        return pltpu.make_async_remote_copy(
            src_ref=total.at[chunk_at(1 - core, way, k)],
            dst_ref=total.at[chunk_at(1 - core, way, k)],
            send_sem=share_send.at[way, k],
            recv_sem=share_recv.at[way, k],
            device_id=(here_t, partner),
            device_id_type=MESH,
        )

    def sends_back(way):
        return (
            (chip <= owner[way]) & (chip > 0),
            (chip >= owner[way]) & (chip < last),
        )

    def send_back(way, k):
        for side in range(2):

            @pl.when(sends_back(way)[side])
            def _():
                back_copy(way, side, k).start()

        share_copy(way, k).start()

    def reduce_chunk(way, k):
        swap_copy(way, k).wait_recv()
        outgoing[way, k] = part[chunk_at(core, way, k), :] + swap[way, k]
        arrives = ((chip > 0) & (chip <= owner[way]), (chip < last) & (chip >= owner[way]))
        for side in range(2):

            @pl.when(arrives[side])
            def _():
                passed_from(way, side, k).wait_recv()
                outgoing[way, k] = outgoing[way, k] + passed[way, side, k]

        @pl.when(chip != owner[way])
        def _():
            pass_copy(way, k).start()

        @pl.when(chip == owner[way])
        def _():
            total[chunk_at(core, way, k), :] = outgoing[way, k]
            send_back(way, k)

    def return_chunk(way, k):
        back_copy(way, 0, k).wait_recv()
        send_back(way, k)

    def chain_step(step):
        for way in range(2):
            hops = jnp.where(
                chip < owner[way], chip, jnp.where(chip > owner[way], last - chip, farthest)
            )
            k = step - hops

            @pl.when((k >= 0) & (k < chunks))
            def _():
                reduce_chunk(way, k)

        for way in range(2):
            away = jnp.where(chip < owner[way], owner[way] - chip, chip - owner[way])
            k = step - farthest - away

            @pl.when((k >= 0) & (k < chunks) & (away > 0))
            def _():
                return_chunk(way, k)

    own_tile.wait()
    tiles = [tile] + [mine.at[step] for step in range(trials_n - 1)]
    for index in range(BANDS):
        for step in range(1, trials_n):
            grad_copy(step, index).wait_recv()
        add_band(part, tiles, index)
        for k in READY[index]:
            for way in range(2):
                swap_copy(way, k).start()
        if index < BANDS - 1:
            for k in READY[index]:
                chain_step(k)

    exponent = jnp.full((1, 1), exponents[setting], jnp.int32)
    damping = jnp.full((1, 1), dampings[setting], F32)
    order_f = exponent.astype(F32)
    ratio = (order_f + 1.0) / order_f
    order = total.shape[1]
    _, pieces = stat_pieces(order)
    weight = 1.0 / (devices * order)

    def begin_root(kind):
        for index in range(BANDS):
            row, col = pieces[kind, index]
            for other in range(index + 1):
                block = total[row : row + band, col + other * band : col + (other + 1) * band]
                block = block * weight
                if other == index:
                    eye = lax.broadcasted_iota(jnp.int32, (band, band), 0) == (
                        lax.broadcasted_iota(jnp.int32, (band, band), 1)
                    )
                    block = block + jnp.where(eye, damping, 0.0)
                stat[index * band : (index + 1) * band, other * band : (other + 1) * band] = block
                if other < index:
                    stat[other * band : (other + 1) * band, index * band : (index + 1) * band] = (
                        block.T
                    )
        norm = jnp.sqrt(jnp.sum(stat[...] * stat[...], keepdims=True) + 1e-06)
        scaling = (1.0 + order_f) / (2.0 * norm)
        stat[...] = stat[...] * (scaling / order_f)
        parts = split(stat[...])
        square[...] = product(parts, parts)
        return jnp.exp(jnp.log(scaling) / order_f)

    def turn_root():
        once = ratio * stat[...] - square[...]
        twice = ratio * once - product(split(stat[...]), split(once))
        turned[...] = jnp.where(exponent == 2, once, twice)

    def end_root(kind):
        short = (2.0 * ratio) * stat[...] - square[...]
        taken = jnp.where(exponent == 4, ratio * short + turned[...], short)
        power = jnp.where(exponent == 4, ratio * ratio * ratio, ratio * ratio)
        rest = product(split(taken), split(turned[...])) - power * turned[...]
        root[kind] = rest - ratio * stat[...]

    sent = [(way, k) for k in range(chunks) for way in range(2)]

    def wait_shared(first, stop):
        for k in range(first, stop):
            for way in range(2):
                shared_by_partner(way, k).wait_recv()

    left_stop = STAT_ENDS[0] + 1
    right_stop = STAT_ENDS[1] + 1
    steps = chunks + 2 * farthest

    @pl.loop(READY[-1][0], left_stop + 2 * farthest)
    def _(step):
        chain_step(step)

    wait_shared(0, left_stop)
    left_scale = begin_root(0)
    chain_step(left_stop + 2 * farthest)
    turn_root()
    chain_step(left_stop + 2 * farthest + 1)
    end_root(0)
    chain_step(steps - 1)
    wait_shared(left_stop, right_stop)
    right_scale = begin_root(1)
    turn_root()
    end_root(1)
    wait_shared(right_stop, chunks)

    average = jnp.concatenate(
        [total[row * band : (row + 1) * band, :] for row in MEAN_BANDS], axis=0
    ) * (1.0 / devices)
    middle = left_scale * (
        ratio * ratio * average + product(split(root[0]), split(average))
    )
    raw = right_scale * (ratio * ratio * middle + product(split(middle), split(root[1])))
    count = order * order
    target = jnp.sqrt(jnp.sum(average * average, keepdims=True) / count)
    spread = jnp.sqrt(jnp.sum(raw * raw, keepdims=True) / count + 1e-06)
    stat[...] = raw * target / spread
    row_share, col_share = out.shape[2:]
    for t in range(trials_n):
        for d in range(data_n):
            finished[t, d] = stat[
                d * row_share : (d + 1) * row_share, t * col_share : (t + 1) * col_share
            ].astype(BF16)

    def block_copy(peer):
        peer_t, peer_d = peer // data_n, lax.rem(peer, data_n)
        return pltpu.make_async_remote_copy(
            src_ref=finished.at[peer_t, peer_d],
            dst_ref=out.at[here_d, here_t],
            send_sem=send_sem.at[peer],
            recv_sem=recv_sem.at[here_d, here_t],
            device_id=(peer_t, peer_d),
            device_id_type=MESH,
        )

    own = pltpu.make_async_copy(finished.at[here_t, here_d], out.at[setting, here_t], own_sem)

    @pl.when(here_d < settings)
    def _():
        own.start()

        @pl.loop(1, devices)
        def _(step):
            block_copy(lax.rem(here + step, devices)).start()

    @pl.loop(0, settings * trials_n)
    def _(source):
        source_t, source_d = source // settings, lax.rem(source, settings)

        @pl.when(source_t * data_n + source_d != here)
        def _():
            pltpu.make_async_remote_copy(
                src_ref=finished.at[here_t, here_d],
                dst_ref=out.at[source_d, source_t],
                send_sem=send_sem.at[here],
                recv_sem=recv_sem.at[source_d, source_t],
                device_id=(source_t, source_d),
                device_id_type=MESH,
            ).wait_recv()

    @pl.when(here_d < settings)
    def _():
        own.wait()

        @pl.loop(1, devices)
        def _(step):
            block_copy(lax.rem(here + step, devices)).wait_send()

    for way, k in sent:
        swap_copy(way, k).wait_send()
        share_copy(way, k).wait_send()

        @pl.when(chip != owner[way])
        def _():
            pass_copy(way, k).wait_send()

        for side in range(2):

            @pl.when(sends_back(way)[side])
            def _():
                back_copy(way, side, k).wait_send()

    for index in range(BANDS):
        for step in range(1, trials_n):
            grad_copy(step, index).wait_send()


def per_device(grads, exponents, dampings):
    trials_n = lax.axis_size("trial")
    data_n = lax.axis_size("dp")
    devices = trials_n * data_n
    settings = exponents.shape[0]
    tiles, order = grads.shape[1], grads.shape[-1]
    assert tiles == trials_n and data_n >= settings and data_n % 2 == 0
    rows = PACKED_BANDS * (order // BANDS)
    size = order // BANDS // 4
    in_vmem = pl.BlockSpec(memory_space=pltpu.VMEM)
    in_smem = pl.BlockSpec(memory_space=pltpu.SMEM)
    in_place = pl.BlockSpec(memory_space=pl.ANY)
    dma = pltpu.SemaphoreType.DMA
    pairs = dma((2, PACKED_BANDS))
    sides = dma((2, 2, PACKED_BANDS))
    whole = pltpu.VMEM((order, order), F32)
    row_share, col_share = order // data_n, order // trials_n

    return pl.pallas_call(
        functools.partial(update_kernel, trials_n, data_n, settings, PACKED_BANDS),
        out_shape=jax.ShapeDtypeStruct((settings, tiles, row_share, col_share), BF16),
        in_specs=[in_place, in_smem, in_smem],
        out_specs=in_vmem,
        scratch_shapes=[
            pltpu.VMEM((order, order), BF16),
            pltpu.VMEM((trials_n - 1, order, order), BF16),
            pltpu.VMEM((rows, order), F32),
            pltpu.VMEM((2, PACKED_BANDS, size, order), F32),
            pltpu.VMEM((2, 2, PACKED_BANDS, size, order), F32),
            pltpu.VMEM((2, PACKED_BANDS, size, order), F32),
            pltpu.VMEM((rows, order), F32),
            whole,
            whole,
            whole,
            pltpu.VMEM((2, order, order), F32),
            pltpu.VMEM((trials_n, data_n, row_share, col_share), BF16),
            dma,
            dma((trials_n - 1, BANDS)),
            dma((trials_n - 1, BANDS)),
            pairs,
            pairs,
            pairs,
            sides,
            sides,
            pairs,
            pairs,
            pairs,
            dma,
            dma((devices,)),
            dma((settings, trials_n)),
        ],
        compiler_params=pltpu.CompilerParams(
            collective_id=0, has_side_effects=True, vmem_limit_bytes=48 * 1024 * 1024
        ),
    )(grads[0], exponents, dampings)


def solution(mesh):
    placed = (P(("trial", "dp"), None, None, None), P(), P())
    return jax.shard_map(
        per_device,
        mesh=mesh,
        in_specs=placed,
        out_specs=P(None, None, "dp", "trial"),
        check_vma=False,
    )
```
